256 devices in a mesh: depth: 8 (over z_lo, y), lat: 32 (over z_hi, x, core).
Axes of the slice: x: 4, y: 4, z: 8 (z_hi: 4, z_lo: 2; z = z_hi * 2 + z_lo), core: 2. Of those that a mesh axis runs over, the one named last changes fastest.
Arguments:
- volume: float32 [64, 1024, 2048], P('depth', 'lat'), may hold values from 0.5 to 2
- measured: float32 [1024, 2048], P('lat'), may hold values from 0.2 to 2
- background: float32 [1024, 2048], P('lat'), may hold values from 0.1 to 1
- point_spread: float32 [64, 25, 25], P('depth'), may hold values from 2.5e-06 to 2.5e-05
Outputs:
- volume_next: float32 [64, 1024, 2048], P('depth', 'lat')
The draws below stay inside these ranges and needn't reach their ends.
All inputs are finite; a program needn't handle non-finite values.
Results may differ from the reference program's by a relative error of at most 0.0001.
Values sent between devices are 32-bit elements; how exact they have to be, the bound alone decides.
A program may use at most 64 MiB of HBM per device.

```python
import math
import jax
import jax.numpy as jnp

PLANES = 64
RADIUS = 12
COLS = 2048
ITERS = 2
ROWS = 1024


def level_of(key, dims, cuts, smallest, top_value):
    factor_of = 1.0
    for dim, blocks in cuts:
        heights = jax.random.uniform(jax.random.fold_in(jax.random.fold_in(key, 6), dim), (blocks,), jnp.float32, smallest / len(cuts), top_value / len(cuts))
        factor_of = factor_of * jnp.repeat(jnp.exp(heights), dims[dim] // blocks).reshape((-1,) + (1,) * (len(dims) - 1 - dim))
    return factor_of


def setup_inputs(seed: int = 0) -> dict:
    key_of = jax.random.split(jax.random.key(seed), 5)
    return {
        "volume": jnp.clip(jnp.exp(math.log(2.0) - 1.3862944 * jax.random.uniform(key_of[0], (PLANES, ROWS, COLS), jnp.float32) ** level_of(key_of[0], (PLANES, ROWS, COLS), ((0, 8), (1, 32)), -0.2, 0.2)), 0.5, 2.0),
        "measured": jnp.clip(jnp.exp(math.log(2.0) - 2.3025851 * jax.random.uniform(key_of[1], (ROWS, COLS), jnp.float32) ** level_of(key_of[1], (ROWS, COLS), ((0, 32),), -0.2, 0.2)), 0.2, 2.0),
        "background": jnp.clip(jnp.exp(math.log(1.0) - 2.3025851 * jax.random.uniform(key_of[2], (ROWS, COLS), jnp.float32) ** level_of(key_of[2], (ROWS, COLS), ((0, 32),), -0.2, 0.2)), 0.1, 1.0),
        "point_spread": jnp.clip(jnp.exp(math.log(2.499999936844688e-05) - 2.3025851 * jax.random.uniform(key_of[3], (PLANES, 2 * RADIUS + 1, 2 * RADIUS + 1), jnp.float32) ** level_of(key_of[3], (PLANES, 2 * RADIUS + 1, 2 * RADIUS + 1), ((0, 8),), -0.2, 0.2)), 2.499999936844688e-06, 2.499999936844688e-05),
    }


def full_conv_sum(images, kernels, out_rows, out_cols):
    spectrum = jnp.fft.rfft2(images, s=(out_rows, out_cols))
    kernel_spec = jnp.fft.rfft2(kernels, s=(out_rows, out_cols))
    return spectrum * kernel_spec


def reference(volume, measured, background, point_spread):
    halo_rows = RADIUS
    full_rows = ROWS + 2 * halo_rows
    full_cols = COLS + 2 * halo_rows
    flipped = point_spread[:, ::-1, ::-1]
    plane_total = jnp.sum(point_spread, axis=(1, 2))
    estimate = volume
    for step in range(ITERS):
        product = full_conv_sum(estimate, flipped, full_rows, full_cols)
        summed = jnp.sum(product, axis=0)
        forward_full = jnp.fft.irfft2(summed, s=(full_rows, full_cols))
        predicted = forward_full[halo_rows:halo_rows + ROWS, halo_rows:halo_rows + COLS] + background
        ratio_img = measured / predicted
        back_spec = full_conv_sum(ratio_img[None], point_spread, full_rows, full_cols)
        back_full = jnp.fft.irfft2(back_spec, s=(full_rows, full_cols))
        backward = back_full[:, halo_rows:halo_rows + ROWS, halo_rows:halo_rows + COLS]
        estimate = estimate * backward / plane_total[:, None, None]
    return estimate
```

```python
import jax
import jax.numpy as jnp
from jax import lax
from jax.experimental import pallas as pl
from jax.experimental.pallas import tpu as pltpu
from jax.sharding import PartitionSpec as P

ITERS = 2
WIDTH = 512
PAD = 32
MESH = pl.DeviceIdType.MESH
bf16, f32 = jnp.bfloat16, jnp.float32


def split(x):
    high = x.astype(bf16)
    return high, (x - high.astype(f32)).astype(bf16)


def dot3(x, w_high, w_low):
    x_high, x_low = split(x) if not isinstance(x, tuple) else x
    dot = lambda a, b: jnp.dot(a, b, preferred_element_type=f32)
    return dot(x_high, w_high[...]) + dot(x_low, w_high[...]) + dot(x_high, w_low[...])


def lanes(rows):
    return lax.broadcasted_iota(jnp.int32, (rows, 128), 1)


def quarters(rows, parts):
    lane = lanes(rows)
    first = jnp.where(lane < 32, parts[0], parts[1])
    return jnp.where(lane < 64, first, jnp.where(lane < 96, parts[2], parts[3]))


def tap_rows(point_spread):
    planes = point_spread.shape[0]
    taps = jnp.pad(point_spread[:, ::-1, :], ((0, 0), (0, 7), (0, 7)))
    return taps.reshape(planes, 32, 8, 4).transpose(3, 0, 2, 1).reshape(4 * planes, 256)


def build_weights(taps, work, fwd_high, fwd_low, adj_high, adj_low):
    rows = taps[...]
    sums = jnp.sum(rows, axis=1, keepdims=True)
    inverse = 1.0 / (sums[0:8] + sums[8:16] + sums[16:24] + sums[24:32])
    for jp in range(32):
        for half in range(2):
            block = jnp.broadcast_to(rows[jp : jp + 1, 128 * half : 128 * half + 128], (8, 128))
            work[8 * jp : 8 * jp + 8, 128 * half : 128 * half + 128] = pltpu.roll(
                block, 0, 1, stride=1, stride_axis=0
            )
    fwd_high[...], fwd_low[...] = split(work[...])
    for jp in range(32):
        p = jp % 8
        work[8 * jp : 8 * jp + 8, :] = work[8 * jp : 8 * jp + 8, :] * inverse[p : p + 1]
    adj_high[...], adj_low[...] = split(work[...].T)


def load_volume(volume, vt, vt_rolled, tile):
    cols = pl.ds(pl.multiple_of(tile * 128, 128), 128)
    rows = pl.ds(pl.multiple_of(tile * 128 + PAD, 8), 128)
    for a in range(2):
        block = jnp.concatenate(
            [volume[p, 8 * rb : 8 * rb + 8, cols] for rb in (2 * a, 2 * a + 1) for p in range(8)], 0
        ).T
        vt[a, rows, :] = block
        vt_rolled[a, rows, :] = pltpu.roll(block, 64, 1)


def forward(k, vt, vt_rolled, w_high, w_low, work, frame):
    rows = WIDTH + 32
    start = k * WIDTH
    lower = lanes(rows) < 64
    groups = [None] * 7
    for rb in range(4):
        a = rb // 2
        low, high = (vt, vt_rolled) if rb % 2 == 0 else (vt_rolled, vt)

        def pair(shift):
            return jnp.where(
                lower,
                low[a, pl.ds(start + 16 + shift, rows), :],
                high[a, pl.ds(start + 17 + shift, rows), :],
            )

        y = dot3(jnp.concatenate([pair(0), pair(2)], 1), w_high, w_low)
        work[rb, 0, 0 : WIDTH + 16, :] = y[: WIDTH + 16, :128] + y[16:, 128:]
        shifted = quarters(WIDTH, [work[rb, 0, o : o + WIDTH, :] for o in (4, 8, 12, 16)]).T
        for g in range(4):
            x = (shifted[8 * g : 8 * g + 8] + shifted[32 + 8 * g : 40 + 8 * g]) + (
                shifted[64 + 8 * g : 72 + 8 * g] + shifted[96 + 8 * g : 104 + 8 * g]
            )
            groups[rb + g] = x if groups[rb + g] is None else groups[rb + g] + x
    frame[4:60, :] = jnp.concatenate(groups, 0)


def load_ratio(ratio, qt, tile, inside):
    cols = pl.ds(pl.multiple_of(tile * 128, 128), 128)
    rows = pl.ds(pl.multiple_of(tile * 128 + PAD, 8), 128)
    x = jnp.where(inside, ratio[4:60, cols], 0.0)
    for rb in range(4):
        y = x[8 * rb : 8 * rb + 32]
        qt[rb, rows, :] = jnp.concatenate([y, y, y, y], 0).T


def adjoint(k, qt, w_high, w_low, work):
    rows = WIDTH + 32
    start = k * WIDTH
    lower = lanes(WIDTH) < 64
    sums = []
    for rb in range(4):
        x = quarters(rows, [qt[rb, pl.ds(start + o, rows), :] for o in (12, 8, 4, 0)])
        both = tuple(jnp.concatenate([h[16:], h[:-16]], 1) for h in split(x))
        z = dot3(both, w_high, w_low)
        work[rb, 0, 0 : WIDTH + 16, :] = z[:, :128]
        work[rb, 1, 0 : WIDTH + 16, :] = z[:, 128:]
        sums.append(
            jnp.where(
                lower,
                work[rb, 0, 16 : 16 + WIDTH, :] + work[rb, 1, 14 : 14 + WIDTH, :],
                work[rb, 0, 15 : 15 + WIDTH, :] + work[rb, 1, 13 : 13 + WIDTH, :],
            )
        )
    return [
        jnp.where(lower, x, y) + pltpu.roll(jnp.where(lower, y, x), 64, 1)
        for x, y in ((sums[0], sums[1]), (sums[2], sums[3]))
    ]


def kernel(
    n_depth, n_lat, chunks,
    volume, measured, background, taps, out,
    vt, vt_rolled, qt, work, w_work, fwd_high, fwd_low, adj_high, adj_low,
    frame, from_next, from_prev, centre, parts, own, ratio,
    halo_send, halo_recv, part_send, part_recv, gather_send, gather_recv, edge_send, edge_recv,
):
    depth, lat = lax.axis_index("depth"), lax.axis_index("lat")
    prev, following = lax.rem(lat + n_lat - 1, n_lat), lax.rem(lat + 1, n_lat)
    half = WIDTH // 2

    barrier = pltpu.get_barrier_semaphore()
    for o in range(1, n_depth):
        pl.semaphore_signal(
            barrier, inc=1, device_id=(lax.rem(depth + o, n_depth), lat), device_id_type=MESH
        )
    for neighbour in (prev, following):
        pl.semaphore_signal(barrier, inc=1, device_id=(depth, neighbour), device_id_type=MESH)

    def region(d, k, row, col):
        return (
            pl.ds(pl.multiple_of(row + 8 * lax.rem(d, 4), 8), 8),
            pl.ds(pl.multiple_of(col + half * (d // 4), half), half),
        )

    def remote(src, dst, send, recv, device):
        return pltpu.make_async_remote_copy(
            src_ref=src, dst_ref=dst, send_sem=send, recv_sem=recv, device_id=device, device_id_type=MESH
        )

    def halo_copies(it, k):
        n = it * chunks + k
        return [
            remote(frame.at[it, k, 0:16], from_next.at[it, k], halo_send.at[n, 0], halo_recv.at[n, 0], (depth, prev)),
            remote(frame.at[it, k, 48:64], from_prev.at[it, k], halo_send.at[n, 1], halo_recv.at[n, 1], (depth, following)),
        ]

    def part_copies(it, k):
        n = it * chunks + k
        copies = []
        for o in range(1, n_depth):
            owner = lax.rem(depth + o, n_depth)
            rows, cols = region(owner, k, 0, 0)
            copies.append(
                remote(centre.at[it, k, rows, cols], parts.at[it, k, o], part_send.at[n, o], part_recv.at[n, o], (owner, lat))
            )
        return copies

    def gather_copies(it, k):
        n = it * chunks + k
        rows, cols = region(depth, k, 16, k * WIDTH)
        return [
            remote(own.at[it, k], ratio.at[it, rows, cols], gather_send.at[n, o], gather_recv.at[n, o], (lax.rem(depth + o, n_depth), lat))
            for o in range(1, n_depth)
        ]

    def edge_copies(it, k):
        n = it * chunks + k
        cols = pl.ds(k * WIDTH, WIDTH)
        return [
            remote(ratio.at[it, 16:32, cols], ratio.at[it, 48:64, cols], edge_send.at[n, 0], edge_recv.at[n, 0], (depth, prev)),
            remote(ratio.at[it, 32:48, cols], ratio.at[it, 0:16, cols], edge_send.at[n, 1], edge_recv.at[n, 1], (depth, following)),
        ]

    def start(copies):
        for copy in copies:
            copy.start()

    def await_arrival(copies):
        for copy in copies:
            copy.wait_recv()

    def scatter_centre(it, k):
        await_arrival(halo_copies(it, k))
        centre[it, k, 0:16] = frame[it, k, 16:32] + jnp.where(lat > 0, from_prev[it, k], 0.0)
        centre[it, k, 16:32] = frame[it, k, 32:48] + jnp.where(lat < n_lat - 1, from_next[it, k], 0.0)
        start(part_copies(it, k))

    def divide(it, k):
        await_arrival(part_copies(it, k))
        rows, cols = region(depth, k, 0, 0)
        total = centre[it, k, rows, cols]
        for o in range(1, n_depth):
            total = total + parts[it, k, o]
        rows, cols = region(depth, k, 0, k * WIDTH)
        value = measured[rows, cols] / (total + background[rows, cols])
        own[it, k] = value
        rows, cols = region(depth, k, 16, k * WIDTH)
        ratio[it, rows, cols] = value
        start(gather_copies(it, k))

    def send_edges(it, k):
        await_arrival(gather_copies(it, k))
        start(edge_copies(it, k))

    frame_row = lax.broadcasted_iota(jnp.int32, (56, 128), 0)
    inside = ((frame_row >= 12) | (lat > 0)) & ((frame_row < 44) | (lat < n_lat - 1))

    def transpose_ratio(it, k):
        await_arrival(edge_copies(it, k))
        for t in range(WIDTH // 128):
            load_ratio(ratio.at[it], qt, k * (WIDTH // 128) + t, inside)

    def update(it, k):
        cols = pl.ds(k * WIDTH, WIDTH)
        rows = pl.ds(k * WIDTH + PAD, WIDTH)
        for a, factor in enumerate(adjoint(k, qt, adj_high, adj_low, work)):
            value = vt[a, rows, :] * factor
            if it < ITERS - 1:
                vt[a, rows, :] = value
                vt_rolled[a, rows, :] = pltpu.roll(value, 64, 1)
            else:
                block = value.T
                for i in range(16):
                    rb, p = 2 * a + i // 8, i % 8
                    out[p, 8 * rb : 8 * rb + 8, cols] = block[8 * i : 8 * i + 8]

    tail = vt.shape[1] - PAD - chunks * WIDTH
    for ref in (vt, vt_rolled, qt):
        ref[:, 0:PAD, :] = jnp.zeros((ref.shape[0], PAD, 128), f32)
        ref[:, PAD + chunks * WIDTH :, :] = jnp.zeros((ref.shape[0], tail, 128), f32)
    for it in range(ITERS):
        for k in range(chunks):
            frame[it, k, 0:8] = jnp.zeros((8, WIDTH), f32)
            frame[it, k, 56:64] = jnp.zeros((8, WIDTH), f32)
    build_weights(taps, w_work, fwd_high, fwd_low, adj_high, adj_low)

    def load_tiles(i, carry):
        for t in range(4):
            load_volume(volume, vt, vt_rolled, 4 * i + t)
        return carry

    lax.fori_loop(0, chunks * WIDTH // 512, load_tiles, 0)

    for it in range(ITERS):
        for k in range(chunks):
            forward(k, vt, vt_rolled, fwd_high, fwd_low, work, frame.at[it, k])
            if it == 0 and k == 0:
                pl.semaphore_wait(barrier, n_depth - 1 + 2)
            start(halo_copies(it, k))
            if k >= 2:
                scatter_centre(it, k - 2)
        scatter_centre(it, 2)
        divide(it, 0)
        scatter_centre(it, 3)
        divide(it, 1)
        send_edges(it, 0)
        divide(it, 2)
        send_edges(it, 1)
        divide(it, 3)
        send_edges(it, 2)
        transpose_ratio(it, 0)
        transpose_ratio(it, 1)
        send_edges(it, 3)
        update(it, 0)
        transpose_ratio(it, 2)
        update(it, 1)
        transpose_ratio(it, 3)
        update(it, 2)
        update(it, 3)

    for it in range(ITERS):
        for k in range(chunks):
            for copies in (halo_copies, part_copies, gather_copies, edge_copies):
                for copy in copies(it, k):
                    copy.wait_send()


def solution(mesh):
    n_depth, n_lat = mesh.shape["depth"], mesh.shape["lat"]

    def on_device(volume, measured, background, point_spread):
        planes, rows, cols = volume.shape
        chunks = cols // WIDTH
        steps = ITERS * chunks
        padded = cols + 2 * PAD
        vmem = lambda *shape, dtype=f32: pltpu.VMEM(shape, dtype)
        dma = lambda n: pltpu.SemaphoreType.DMA((steps, n))
        return pl.pallas_call(
            lambda *refs: kernel(n_depth, n_lat, chunks, *refs),
            out_shape=jax.ShapeDtypeStruct(volume.shape, f32),
            in_specs=[pl.BlockSpec(memory_space=pltpu.VMEM)] * 4,
            out_specs=pl.BlockSpec(memory_space=pltpu.VMEM),
            scratch_shapes=[
                vmem(2, padded, 128),
                vmem(2, padded, 128),
                vmem(4, padded, 128),
                vmem(4, 2, WIDTH + 32, 128),
                vmem(256, 256),
                vmem(256, 256, dtype=bf16),
                vmem(256, 256, dtype=bf16),
                vmem(256, 256, dtype=bf16),
                vmem(256, 256, dtype=bf16),
                vmem(ITERS, chunks, 64, WIDTH),
                vmem(ITERS, chunks, 16, WIDTH),
                vmem(ITERS, chunks, 16, WIDTH),
                vmem(ITERS, chunks, rows, WIDTH),
                vmem(ITERS, chunks, n_depth, 8, WIDTH // 2),
                vmem(ITERS, chunks, 8, WIDTH // 2),
                vmem(ITERS, 64, cols),
                dma(2), dma(2), dma(n_depth), dma(n_depth), dma(n_depth), dma(n_depth), dma(2), dma(2),
            ],
            compiler_params=pltpu.CompilerParams(
                collective_id=0, has_side_effects=True, vmem_limit_bytes=56 << 20
            ),
            cost_estimate=pl.CostEstimate(
                flops=2 * 3 * 4 * 4 * 2048 * 256 * 256, bytes_accessed=5 << 20, transcendentals=0
            ),
            name="deconvolve",
        )(volume, measured, background, tap_rows(point_spread))

    return jax.shard_map(
        on_device,
        mesh=mesh,
        in_specs=(P("depth", "lat", None), P("lat", None), P("lat", None), P("depth", None, None)),
        out_specs=P("depth", "lat", None),
        check_vma=False,
    )
```

```python
import jax
import jax.numpy as jnp
from jax import lax
from jax.experimental import pallas as pl
from jax.experimental.pallas import tpu as pltpu
from jax.sharding import PartitionSpec as P

ITERS = 2
WIDTH = 512
PAD = 32
MESH = pl.DeviceIdType.MESH
bf16, f32 = jnp.bfloat16, jnp.float32


def split(x):
    high = x.astype(bf16)
    return high, (x - high.astype(f32)).astype(bf16)


def dot3(x, w_high, w_low):
    x_high, x_low = split(x) if not isinstance(x, tuple) else x
    dot = lambda a, b: jnp.dot(a, b, preferred_element_type=f32)
    return dot(x_high, w_high[...]) + dot(x_low, w_high[...]) + dot(x_high, w_low[...])


def lanes(rows):
    return lax.broadcasted_iota(jnp.int32, (rows, 128), 1)


def quarters(rows, parts):
    lane = lanes(rows)
    first = jnp.where(lane < 32, parts[0], parts[1])
    return jnp.where(lane < 64, first, jnp.where(lane < 96, parts[2], parts[3]))


def build_weights(point_spread, taps, work, fwd_high, fwd_low, adj_high, adj_low):
    count, planes, _ = point_spread.shape
    taps[...] = jnp.zeros_like(taps)
    for a in range(count):
        taps[8 * a : 8 * a + 8, 0:count] = point_spread[a]
    row = lax.broadcasted_iota(jnp.int32, (256, 256), 0)
    col = lax.broadcasted_iota(jnp.int32, (256, 256), 1)
    flip = (row % 8 == col // 32) & (row // 8 + col % 32 == count - 1)
    flipped = lax.dot_general(
        taps[:, 0:32], flip.astype(f32), (((0,), (0,)), ((), ())),
        precision=lax.Precision.HIGHEST, preferred_element_type=f32,
    )
    column_sums = jnp.sum(flipped, axis=0, keepdims=True)
    lane = lanes(8)
    for j in range(4):
        for p in range(planes):
            half = slice(128 * (p // 4), 128 * (p // 4) + 128)
            rows = slice(8 * (planes * j + p), 8 * (planes * j + p) + 8)
            for h in range(2):
                block = jnp.zeros((8, 128), f32)
                for g in range(4 * h, min(4 * h + 4, 7)):
                    source = jnp.broadcast_to(flipped[4 * g + j : 4 * g + j + 1, half], (8, 128))
                    moved = pltpu.roll(source, 32 * (g - p) % 128, 1, stride=1, stride_axis=0)
                    block = jnp.where(lane // 32 == g % 4, moved, block)
                work[rows, 128 * h : 128 * h + 128] = block
    fwd_high[...], fwd_low[...] = split(work[...])
    for p in range(planes):
        inverse = 1.0 / jnp.sum(column_sums[:, 32 * p : 32 * p + 32], axis=1, keepdims=True)
        for j in range(4):
            rows = slice(8 * (planes * j + p), 8 * (planes * j + p) + 8)
            work[rows, :] = work[rows, :] * inverse
    adj_high[...], adj_low[...] = split(work[...].T)


def load_volume(volume, vt, vt_rolled, tile):
    cols = pl.ds(pl.multiple_of(tile * 128, 128), 128)
    rows = pl.ds(pl.multiple_of(tile * 128 + PAD, 8), 128)
    for a in range(2):
        block = jnp.concatenate(
            [volume[p, 8 * rb : 8 * rb + 8, cols] for rb in (2 * a, 2 * a + 1) for p in range(8)], 0
        ).T
        vt[a, rows, :] = block
        vt_rolled[a, rows, :] = pltpu.roll(block, 64, 1)


def forward(k, vt, vt_rolled, w_high, w_low, work, frame):
    rows = WIDTH + 32
    start = k * WIDTH
    lower = lanes(rows) < 64
    groups = [None] * 7
    for rb in range(4):
        a = rb // 2
        low, high = (vt, vt_rolled) if rb % 2 == 0 else (vt_rolled, vt)

        def pair(shift):
            return jnp.where(
                lower,
                low[a, pl.ds(start + 16 + shift, rows), :],
                high[a, pl.ds(start + 17 + shift, rows), :],
            )

        y = dot3(jnp.concatenate([pair(0), pair(2)], 1), w_high, w_low)
        work[rb, 0, 0 : WIDTH + 16, :] = y[: WIDTH + 16, :128] + y[16:, 128:]
        shifted = quarters(WIDTH, [work[rb, 0, o : o + WIDTH, :] for o in (4, 8, 12, 16)]).T
        for g in range(4):
            x = (shifted[8 * g : 8 * g + 8] + shifted[32 + 8 * g : 40 + 8 * g]) + (
                shifted[64 + 8 * g : 72 + 8 * g] + shifted[96 + 8 * g : 104 + 8 * g]
            )
            groups[rb + g] = x if groups[rb + g] is None else groups[rb + g] + x
    frame[0:56, :] = jnp.concatenate(groups, 0)
    frame[56:64, :] = jnp.zeros((8, WIDTH), f32)


def load_ratio(ratio, qt, tile, inside):
    cols = pl.ds(pl.multiple_of(tile * 128, 128), 128)
    rows = pl.ds(pl.multiple_of(tile * 128 + PAD, 8), 128)
    x = jnp.where(inside, ratio[0:56, cols], 0.0)
    for rb in range(4):
        y = x[8 * rb : 8 * rb + 32]
        qt[rb, rows, :] = jnp.concatenate([y, y, y, y], 0).T


def adjoint(k, qt, w_high, w_low, work):
    rows = WIDTH + 32
    start = k * WIDTH
    lower = lanes(WIDTH) < 64
    sums = []
    for rb in range(4):
        x = quarters(rows, [qt[rb, pl.ds(start + o, rows), :] for o in (12, 8, 4, 0)])
        both = tuple(jnp.concatenate([h[16:], h[:-16]], 1) for h in split(x))
        z = dot3(both, w_high, w_low)
        work[rb, 0, 0 : WIDTH + 16, :] = z[:, :128]
        work[rb, 1, 0 : WIDTH + 16, :] = z[:, 128:]
        sums.append(
            jnp.where(
                lower,
                work[rb, 0, 16 : 16 + WIDTH, :] + work[rb, 1, 14 : 14 + WIDTH, :],
                work[rb, 0, 15 : 15 + WIDTH, :] + work[rb, 1, 13 : 13 + WIDTH, :],
            )
        )
    return [
        jnp.where(lower, x, y) + pltpu.roll(jnp.where(lower, y, x), 64, 1)
        for x, y in ((sums[0], sums[1]), (sums[2], sums[3]))
    ]


def kernel(
    n_depth, n_lat, chunks,
    volume_hbm, measured_hbm, background_hbm, point_spread, out_hbm,
    volume, vt, vt_rolled, qt, work, taps, w_work, fwd_high, fwd_low, adj_high, adj_low,
    frame, from_next, from_prev, total, parts, own, ratio, images, images_halo, mine, out,
    load_sem, image_sem, store_sem, image_send, image_recv, halo_send, halo_recv, part_send, part_recv, gather_send, gather_recv,
):
    depth, lat = lax.axis_index("depth"), lax.axis_index("lat")
    prev, following = lax.rem(lat + n_lat - 1, n_lat), lax.rem(lat + 1, n_lat)
    has_next, has_prev = lat < n_lat - 1, lat > 0

    barrier = pltpu.get_barrier_semaphore()
    for row in (prev, following):
        pl.semaphore_signal(barrier, inc=1, device_id=(depth, row), device_id_type=MESH)
    for o in range(1, n_depth):
        pl.semaphore_signal(
            barrier, inc=1, device_id=(lax.rem(depth + o, n_depth), lat), device_id_type=MESH
        )

    def columns(k):
        return pl.ds(k * WIDTH, WIDTH)

    def group(d):
        return pl.ds(pl.multiple_of(8 * d, 8), 8)

    def loads(k):
        return pltpu.make_async_copy(volume_hbm.at[:, :, columns(k)], volume.at[:, :, columns(k)], load_sem.at[k])

    def image_loads():
        return [
            pltpu.make_async_copy(image, images.at[i], image_sem.at[i])
            for i, image in enumerate((measured_hbm, background_hbm))
        ]

    def stores(k):
        return pltpu.make_async_copy(out.at[:, :, columns(k)], out_hbm.at[:, :, columns(k)], store_sem.at[k])

    for k in range(chunks):
        loads(k).start()
    for copy in image_loads():
        copy.start()

    def remote(src, dst, send, recv, device):
        return pltpu.make_async_remote_copy(
            src_ref=src, dst_ref=dst, send_sem=send, recv_sem=recv, device_id=device, device_id_type=MESH
        )

    def image_copies(rows, neighbour):
        return [
            remote(images.at[i, rows], images_halo.at[i], image_send.at[i], image_recv.at[i], (depth, neighbour))
            for i in range(2)
        ]

    needs_prev = depth <= 1
    needs_next = (depth == 5) | (depth == 6)

    def each_image(action):
        @pl.when(needs_prev)
        def _():
            for copy in image_copies(slice(16, 32), following):
                action(copy)

        @pl.when(needs_next)
        def _():
            for copy in image_copies(slice(0, 16), prev):
                action(copy)

    def gather_images():
        each_image(lambda copy: copy.wait_recv())
        for g in range(n_depth):

            @pl.when(depth == g)
            def _(g=g):
                for i in range(2):
                    if g == 0:
                        mine[i] = images_halo[i, 4:12]
                    elif g == 1:
                        mine[i, 0:4] = images_halo[i, 12:16]
                        mine[i, 4:8] = images[i, 0:4]
                    elif g == 5:
                        mine[i, 0:4] = images[i, 28:32]
                        mine[i, 4:8] = images_halo[i, 0:4]
                    elif g == 6:
                        mine[i] = images_halo[i, 4:12]
                    elif g == 7:
                        mine[i] = images[i, 0:8]
                    else:
                        mine[i] = images[i, 8 * g - 12 : 8 * g - 4]

    def halo_copy(it, k, up):
        n = it * chunks + k
        if up:
            return remote(frame.at[it, k, 0:24], from_next.at[it, k], halo_send.at[n, 0], halo_recv.at[n, 0], (depth, prev))
        return remote(frame.at[it, k, 32:56], from_prev.at[it, k], halo_send.at[n, 1], halo_recv.at[n, 1], (depth, following))

    def peer(o):
        return (lax.rem(depth + o, n_depth), lat)

    def part_copy(it, k, o):
        n = it * chunks + k
        owner, _ = peer(o)
        return remote(total.at[it, k, group(owner)], parts.at[it, k, o], part_send.at[n], part_recv.at[n], peer(o))

    def gather_copy(it, k, o):
        n = it * chunks + k
        return remote(own.at[it, k], ratio.at[it, group(depth), columns(k)], gather_send.at[n], gather_recv.at[n], peer(o))

    def all_of(it, k, send, recv):
        n = it * chunks + k
        every = parts.at[it, k, 1:n_depth]
        return remote(every, every, send.at[n], recv.at[n], peer(1))

    def halos(it, k, action):
        @pl.when(has_next)
        def _():
            action(halo_copy(it, k, False))

        @pl.when(has_prev)
        def _():
            action(halo_copy(it, k, True))

    def send_halos(it, k):
        halos(it, k, lambda copy: copy.start())

    def send_parts(it, k):
        total[it, k] = frame[it, k]

        @pl.when(has_prev)
        def _():
            halo_copy(it, k, False).wait_recv()
            total[it, k, 0:24] = total[it, k, 0:24] + from_prev[it, k]

        @pl.when(has_next)
        def _():
            halo_copy(it, k, True).wait_recv()
            total[it, k, 32:56] = total[it, k, 32:56] + from_next[it, k]

        for o in range(1, n_depth):
            part_copy(it, k, o).start()

    def await_part_sends(it, k):
        halos(it, k, lambda copy: copy.wait_send())
        all_of(it, k, part_send, part_recv).wait_send()

    def await_gather_sends(it, k):
        all_of(it, k, gather_send, gather_recv).wait_send()

    def divide(it, k):
        all_of(it, k, part_send, part_recv).wait_recv()
        rows = group(depth)
        value = total[it, k, rows]
        for o in range(1, n_depth):
            value = value + parts[it, k, o]
        value = mine[0, :, columns(k)] / (value + mine[1, :, columns(k)])
        own[it, k] = value
        for o in range(1, n_depth):
            gather_copy(it, k, o).start()
        ratio[it, rows, columns(k)] = value

    frame_row = lax.broadcasted_iota(jnp.int32, (56, 128), 0)
    inside = ((frame_row >= 12) | (lat > 0)) & ((frame_row < 44) | (lat < n_lat - 1))

    def await_ratio(it, k):
        all_of(it, k, gather_send, gather_recv).wait_recv()

    def transpose_ratio(it, k):
        for t in range(WIDTH // 128):
            load_ratio(ratio.at[it], qt, k * (WIDTH // 128) + t, inside)

    def update(it, k):
        rows = pl.ds(k * WIDTH + PAD, WIDTH)
        for a, factor in enumerate(adjoint(k, qt, adj_high, adj_low, work)):
            value = vt[a, rows, :] * factor
            if it < ITERS - 1:
                vt[a, rows, :] = value
                vt_rolled[a, rows, :] = pltpu.roll(value, 64, 1)
            else:
                block = value.T
                for i in range(16):
                    rb, p = 2 * a + i // 8, i % 8
                    out[p, 8 * rb : 8 * rb + 8, columns(k)] = block[8 * i : 8 * i + 8]
        if it == ITERS - 1:
            stores(k).start()

    build_weights(point_spread, taps, w_work, fwd_high, fwd_low, adj_high, adj_low)
    tail = vt.shape[1] - PAD - chunks * WIDTH
    for ref in (vt, vt_rolled, qt):
        ref[:, 0:PAD, :] = jnp.zeros((ref.shape[0], PAD, 128), f32)
        ref[:, PAD + chunks * WIDTH :, :] = jnp.zeros((ref.shape[0], tail, 128), f32)

    def transpose_volume(k):
        for t in range(WIDTH // 128):
            load_volume(volume, vt, vt_rolled, k * (WIDTH // 128) + t)

    for copy in image_loads():
        copy.wait()
    for k in range(chunks):
        loads(k).wait()
    for k in range(2):
        transpose_volume(k)

    for it in range(ITERS):
        for k in range(chunks):
            forward(k, vt, vt_rolled, fwd_high, fwd_low, work, frame.at[it, k])
            if it == 0 and k + 2 < chunks:
                transpose_volume(k + 2)
            if it == 0 and k == 0:
                pl.semaphore_wait(barrier, n_depth + 1)
            send_halos(it, k)
            if it == 0 and k == 0:
                each_image(lambda copy: copy.start())
            if k >= 2:
                send_parts(it, k - 2)
        for k in range(chunks - 2, chunks):
            send_parts(it, k)
        if it == 0:
            gather_images()
        else:
            for k in range(chunks):
                await_part_sends(it - 1, k)
                await_gather_sends(it - 1, k)
        for k in range(chunks):
            divide(it, k)
        if it == ITERS - 1:
            each_image(lambda copy: copy.wait_send())
            for k in range(chunks):
                await_part_sends(it, k)
        await_ratio(it, 0)
        transpose_ratio(it, 0)
        for k in range(chunks):
            if k + 1 < chunks:
                await_ratio(it, k + 1)
                transpose_ratio(it, k + 1)
            update(it, k)

    for k in range(chunks):
        await_gather_sends(ITERS - 1, k)
    for k in range(chunks):
        stores(k).wait()


def solution(mesh):
    n_depth, n_lat = mesh.shape["depth"], mesh.shape["lat"]

    def on_device(volume, measured, background, point_spread):
        planes, rows, cols = volume.shape
        chunks = cols // WIDTH
        steps = ITERS * chunks
        padded = cols + 2 * PAD
        vmem = lambda *shape, dtype=f32: pltpu.VMEM(shape, dtype)
        dma = lambda *shape: pltpu.SemaphoreType.DMA(shape)
        return pl.pallas_call(
            lambda *refs: kernel(n_depth, n_lat, chunks, *refs),
            out_shape=jax.ShapeDtypeStruct(volume.shape, f32),
            in_specs=[pl.BlockSpec(memory_space=pl.ANY)] * 3 + [pl.BlockSpec(memory_space=pltpu.VMEM)],
            out_specs=pl.BlockSpec(memory_space=pl.ANY),
            scratch_shapes=[
                vmem(planes, rows, cols),
                vmem(2, padded, 128),
                vmem(2, padded, 128),
                vmem(4, padded, 128),
                vmem(4, 2, WIDTH + 32, 128),
                vmem(256, 128),
                vmem(256, 256),
                vmem(256, 256, dtype=bf16),
                vmem(256, 256, dtype=bf16),
                vmem(256, 256, dtype=bf16),
                vmem(256, 256, dtype=bf16),
                vmem(ITERS, chunks, 64, WIDTH),
                vmem(ITERS, chunks, 24, WIDTH),
                vmem(ITERS, chunks, 24, WIDTH),
                vmem(ITERS, chunks, 64, WIDTH),
                vmem(ITERS, chunks, n_depth, 8, WIDTH),
                vmem(ITERS, chunks, 8, WIDTH),
                vmem(ITERS, 64, cols),
                vmem(2, rows, cols),
                vmem(2, 16, cols),
                vmem(2, 8, cols),
                vmem(planes, rows, cols),
                dma(chunks), dma(2), dma(chunks), dma(2), dma(2),
                dma(steps, 2), dma(steps, 2), dma(steps), dma(steps), dma(steps), dma(steps),
            ],
            compiler_params=pltpu.CompilerParams(
                collective_id=0, has_side_effects=True, vmem_limit_bytes=60 << 20
            ),
            cost_estimate=pl.CostEstimate(
                flops=2 * 3 * 4 * 4 * 2048 * 256 * 256, bytes_accessed=5 << 20, transcendentals=0
            ),
            name="deconvolve",
        )(volume, measured, background, point_spread.transpose(1, 0, 2))

    return jax.shard_map(
        on_device,
        mesh=mesh,
        in_specs=(P("depth", "lat", None), P("lat", None), P("lat", None), P("depth", None, None)),
        out_specs=P("depth", "lat", None),
        check_vma=False,
    )
```

```python
import jax
import jax.numpy as jnp
from jax import lax
from jax.experimental import pallas as pl
from jax.experimental.pallas import tpu as pltpu
from jax.sharding import PartitionSpec as P

ITERS = 2
WIDTH = 512
PAD = 32
MESH = pl.DeviceIdType.MESH
bf16, f32 = jnp.bfloat16, jnp.float32


def split(x):
    high = x.astype(bf16)
    return high, (x - high.astype(f32)).astype(bf16)


def dot3(x, w_high, w_low):
    x_high, x_low = split(x) if not isinstance(x, tuple) else x
    dot = lambda a, b: jnp.dot(a, b, preferred_element_type=f32)
    return dot(x_high, w_high[...]) + dot(x_low, w_high[...]) + dot(x_high, w_low[...])


def lanes(rows):
    return lax.broadcasted_iota(jnp.int32, (rows, 128), 1)


def quarters(rows, parts):
    lane = lanes(rows)
    first = jnp.where(lane < 32, parts[0], parts[1])
    return jnp.where(lane < 64, first, jnp.where(lane < 96, parts[2], parts[3]))


def build_weights(point_spread, taps, work, fwd_high, fwd_low, adj_high, adj_low):
    count, planes, _ = point_spread.shape
    taps[...] = jnp.zeros_like(taps)
    for a in range(count):
        taps[8 * a : 8 * a + 8, 0:count] = point_spread[a]
    row = lax.broadcasted_iota(jnp.int32, (256, 256), 0)
    col = lax.broadcasted_iota(jnp.int32, (256, 256), 1)
    flip = (row % 8 == col // 32) & (row // 8 + col % 32 == count - 1)
    flipped = lax.dot_general(
        taps[:, 0:32], flip.astype(f32), (((0,), (0,)), ((), ())),
        precision=lax.Precision.HIGHEST, preferred_element_type=f32,
    )
    column_sums = jnp.sum(flipped, axis=0, keepdims=True)
    lane = lanes(8)
    for j in range(4):
        for p in range(planes):
            half = slice(128 * (p // 4), 128 * (p // 4) + 128)
            rows = slice(8 * (planes * j + p), 8 * (planes * j + p) + 8)
            for h in range(2):
                block = jnp.zeros((8, 128), f32)
                for g in range(4 * h, min(4 * h + 4, 7)):
                    source = jnp.broadcast_to(flipped[4 * g + j : 4 * g + j + 1, half], (8, 128))
                    moved = pltpu.roll(source, 32 * (g - p) % 128, 1, stride=1, stride_axis=0)
                    block = jnp.where(lane // 32 == g % 4, moved, block)
                work[rows, 128 * h : 128 * h + 128] = block
    fwd_high[...], fwd_low[...] = split(work[...])
    for p in range(planes):
        inverse = 1.0 / jnp.sum(column_sums[:, 32 * p : 32 * p + 32], axis=1, keepdims=True)
        for j in range(4):
            rows = slice(8 * (planes * j + p), 8 * (planes * j + p) + 8)
            work[rows, :] = work[rows, :] * inverse
    adj_high[...], adj_low[...] = split(work[...].T)


def load_volume(volume, vt, vt_rolled, tile):
    cols = pl.ds(pl.multiple_of(tile * 128, 128), 128)
    rows = pl.ds(pl.multiple_of(tile * 128 + PAD, 8), 128)
    for a in range(2):
        block = jnp.concatenate(
            [volume[p, 8 * rb : 8 * rb + 8, cols] for rb in (2 * a, 2 * a + 1) for p in range(8)], 0
        ).T
        vt[a, rows, :] = block
        vt_rolled[a, rows, :] = pltpu.roll(block, 64, 1)


def forward(k, vt, vt_rolled, w_high, w_low, work, frame):
    rows = WIDTH + 32
    start = k * WIDTH
    lower = lanes(rows) < 64
    groups = [None] * 7
    for rb in range(4):
        a = rb // 2
        low, high = (vt, vt_rolled) if rb % 2 == 0 else (vt_rolled, vt)

        def pair(shift):
            return jnp.where(
                lower,
                low[a, pl.ds(start + 16 + shift, rows), :],
                high[a, pl.ds(start + 17 + shift, rows), :],
            )

        y = dot3(jnp.concatenate([pair(0), pair(2)], 1), w_high, w_low)
        work[rb, 0, 0 : WIDTH + 16, :] = y[: WIDTH + 16, :128] + y[16:, 128:]
        shifted = quarters(WIDTH, [work[rb, 0, o : o + WIDTH, :] for o in (4, 8, 12, 16)]).T
        for g in range(4):
            x = (shifted[8 * g : 8 * g + 8] + shifted[32 + 8 * g : 40 + 8 * g]) + (
                shifted[64 + 8 * g : 72 + 8 * g] + shifted[96 + 8 * g : 104 + 8 * g]
            )
            groups[rb + g] = x if groups[rb + g] is None else groups[rb + g] + x
    frame[0:56, :] = jnp.concatenate(groups, 0)
    frame[56:64, :] = jnp.zeros((8, WIDTH), f32)


def load_ratio(ratio, qt, tile, inside):
    cols = pl.ds(pl.multiple_of(tile * 128, 128), 128)
    rows = pl.ds(pl.multiple_of(tile * 128 + PAD, 8), 128)
    x = jnp.where(inside, ratio[0:56, cols], 0.0)
    for rb in range(4):
        y = x[8 * rb : 8 * rb + 32]
        qt[rb, rows, :] = jnp.concatenate([y, y, y, y], 0).T


def adjoint(start, width, qt, w_high, w_low, work):
    rows = width + 32
    lower = lanes(width) < 64
    sums = []
    for rb in range(4):
        x = quarters(rows, [qt[rb, pl.ds(start + o, rows), :] for o in (12, 8, 4, 0)])
        both = tuple(jnp.concatenate([h[16:], h[:-16]], 1) for h in split(x))
        z = dot3(both, w_high, w_low)
        work[rb, 0, 0 : width + 16, :] = z[:, :128]
        work[rb, 1, 0 : width + 16, :] = z[:, 128:]
        sums.append(
            jnp.where(
                lower,
                work[rb, 0, 16 : 16 + width, :] + work[rb, 1, 14 : 14 + width, :],
                work[rb, 0, 15 : 15 + width, :] + work[rb, 1, 13 : 13 + width, :],
            )
        )
    return [
        jnp.where(lower, x, y) + pltpu.roll(jnp.where(lower, y, x), 64, 1)
        for x, y in ((sums[0], sums[1]), (sums[2], sums[3]))
    ]


def kernel(
    n_depth, n_lat, chunks,
    volume_hbm, measured_hbm, background_hbm, point_spread, out_hbm,
    volume, vt, vt_rolled, qt, work, taps, w_work, fwd_high, fwd_low, adj_high, adj_low,
    frame, from_next, from_prev, total, parts, own, ratio, images, images_edge, images_halo, mine, out,
    load_sem, image_sem, store_sem, image_send, image_recv, halo_send, halo_recv, part_send, part_recv, gather_send, gather_recv,
):
    depth, lat = lax.axis_index("depth"), lax.axis_index("lat")
    prev, following = lax.rem(lat + n_lat - 1, n_lat), lax.rem(lat + 1, n_lat)
    has_next, has_prev = lat < n_lat - 1, lat > 0

    barrier = pltpu.get_barrier_semaphore()
    for row in (prev, following):
        pl.semaphore_signal(barrier, inc=1, device_id=(depth, row), device_id_type=MESH)
    for o in range(1, n_depth):
        pl.semaphore_signal(
            barrier, inc=1, device_id=(lax.rem(depth + o, n_depth), lat), device_id_type=MESH
        )

    def columns(k):
        return pl.ds(k * WIDTH, WIDTH)

    def group(d):
        return pl.ds(pl.multiple_of(8 * d, 8), 8)

    def loads(k):
        return pltpu.make_async_copy(volume_hbm.at[:, :, columns(k)], volume.at[:, :, columns(k)], load_sem.at[k])

    def image_loads():
        return [
            pltpu.make_async_copy(image, images.at[i], image_sem.at[i])
            for i, image in enumerate((measured_hbm, background_hbm))
        ]

    def stores(k):
        first, end = store_range(k)
        cols = pl.ds(first, end - first)
        return pltpu.make_async_copy(out.at[:, :, cols], out_hbm.at[:, :, cols], store_sem.at[k])

    for k in range(chunks):
        loads(k).start()
    for copy in image_loads():
        copy.start()

    def remote(src, dst, send, recv, device):
        return pltpu.make_async_remote_copy(
            src_ref=src, dst_ref=dst, send_sem=send, recv_sem=recv, device_id=device, device_id_type=MESH
        )

    def each_image(action):
        for g, count, neighbour in ((0, 2, following), (1, 1, following), (5, 1, prev), (6, 2, prev)):

            @pl.when(depth == g)
            def _(count=count, neighbour=neighbour):
                action(
                    remote(
                        images_edge.at[0:count], images_halo.at[0:count],
                        image_send, image_recv, (depth, neighbour),
                    )
                )

    def pack_images():
        for g, first, count in ((0, 20, 8), (1, 28, 4), (5, 0, 4), (6, 4, 8)):

            @pl.when(depth == g)
            def _(first=first, count=count):
                for i in range(2):
                    rows = images[i, first : first + count]
                    if count == 8:
                        images_edge[i] = rows
                    else:
                        images_edge[0, 4 * i : 4 * i + 4] = rows

    def gather_images():
        each_image(lambda copy: copy.wait_recv())
        for g in range(n_depth):

            @pl.when(depth == g)
            def _(g=g):
                for i in range(2):
                    if g in (0, 6):
                        mine[i] = images_halo[i]
                    elif g == 1:
                        mine[i, 0:4] = images_halo[0, 4 * i : 4 * i + 4]
                        mine[i, 4:8] = images[i, 0:4]
                    elif g == 5:
                        mine[i, 0:4] = images[i, 28:32]
                        mine[i, 4:8] = images_halo[0, 4 * i : 4 * i + 4]
                    elif g == 7:
                        mine[i] = images[i, 0:8]
                    else:
                        mine[i] = images[i, 8 * g - 12 : 8 * g - 4]

    def halo_copy(it, k, up):
        n = it * chunks + k
        if up:
            return remote(frame.at[it, k, 0:24], from_next.at[it, k], halo_send.at[n, 0], halo_recv.at[n, 0], (depth, prev))
        return remote(frame.at[it, k, 32:56], from_prev.at[it, k], halo_send.at[n, 1], halo_recv.at[n, 1], (depth, following))

    def peer(o):
        return (lax.rem(depth + o, n_depth), lat)

    def part_copy(it, k, o):
        n = it * chunks + k
        owner, _ = peer(o)
        return remote(total.at[it, k, group(owner)], parts.at[it, k, o], part_send.at[n], part_recv.at[n], peer(o))

    def gather_copy(it, k, o):
        n = it * chunks + k
        return remote(own.at[it, k], ratio.at[it, group(depth), columns(k)], gather_send.at[n], gather_recv.at[n], peer(o))

    def all_of(it, k, send, recv):
        n = it * chunks + k
        every = parts.at[it, k, 1:n_depth]
        return remote(every, every, send.at[n], recv.at[n], peer(1))

    def halos(it, k, action):
        @pl.when(has_next)
        def _():
            action(halo_copy(it, k, False))

        @pl.when(has_prev)
        def _():
            action(halo_copy(it, k, True))

    def send_halos(it, k):
        halos(it, k, lambda copy: copy.start())

    def send_parts(it, k):
        total[it, k] = frame[it, k]

        @pl.when(has_prev)
        def _():
            halo_copy(it, k, False).wait_recv()
            total[it, k, 0:24] = total[it, k, 0:24] + from_prev[it, k]

        @pl.when(has_next)
        def _():
            halo_copy(it, k, True).wait_recv()
            total[it, k, 32:56] = total[it, k, 32:56] + from_next[it, k]

        for o in range(1, n_depth):
            part_copy(it, k, o).start()

    def await_part_sends(it, k):
        halos(it, k, lambda copy: copy.wait_send())
        all_of(it, k, part_send, part_recv).wait_send()

    def await_gather_sends(it, k):
        all_of(it, k, gather_send, gather_recv).wait_send()

    def divide(it, k):
        all_of(it, k, part_send, part_recv).wait_recv()
        rows = group(depth)
        value = total[it, k, rows]
        for o in range(1, n_depth):
            value = value + parts[it, k, o]
        value = mine[0, :, columns(k)] / (value + mine[1, :, columns(k)])
        own[it, k] = value
        for o in range(1, n_depth):
            gather_copy(it, k, o).start()
        ratio[it, rows, columns(k)] = value

    frame_row = lax.broadcasted_iota(jnp.int32, (56, 128), 0)
    inside = ((frame_row >= 12) | (lat > 0)) & ((frame_row < 44) | (lat < n_lat - 1))

    def await_ratio(it, k):
        all_of(it, k, gather_send, gather_recv).wait_recv()

    def transpose_ratio(it, k):
        for t in range(WIDTH // 128):
            load_ratio(ratio.at[it], qt, k * (WIDTH // 128) + t, inside)

    def update_range(k):
        return max(k * WIDTH - 16, 0), (k + 1) * WIDTH - (16 if k + 1 < chunks else 0)

    def store_range(k):
        first, end = update_range(k)
        return first // 128 * 128, end // 128 * 128

    def update(it, k):
        first, end = update_range(k)
        rows = pl.ds(first + PAD, end - first)
        for a, factor in enumerate(adjoint(first, end - first, qt, adj_high, adj_low, work)):
            value = vt[a, rows, :] * factor
            vt[a, rows, :] = value
            if it < ITERS - 1:
                vt_rolled[a, rows, :] = pltpu.roll(value, 64, 1)
        if it == ITERS - 1:
            first, end = store_range(k)
            for a in range(2):
                block = vt[a, first + PAD : end + PAD, :].T
                for i in range(16):
                    rb, p = 2 * a + i // 8, i % 8
                    out[p, 8 * rb : 8 * rb + 8, first:end] = block[8 * i : 8 * i + 8]
            stores(k).start()

    build_weights(point_spread, taps, w_work, fwd_high, fwd_low, adj_high, adj_low)
    tail = vt.shape[1] - PAD - chunks * WIDTH
    for ref in (vt, vt_rolled, qt):
        ref[:, 0:PAD, :] = jnp.zeros((ref.shape[0], PAD, 128), f32)
        ref[:, PAD + chunks * WIDTH :, :] = jnp.zeros((ref.shape[0], tail, 128), f32)

    def transpose_volume(k):
        for t in range(WIDTH // 128):
            load_volume(volume, vt, vt_rolled, k * (WIDTH // 128) + t)

    for copy in image_loads():
        copy.wait()
    pack_images()
    for k in range(chunks):
        loads(k).wait()
    for k in range(2):
        transpose_volume(k)

    def predict(it, k):
        forward(k, vt, vt_rolled, fwd_high, fwd_low, work, frame.at[it, k])

    last = chunks - 1
    for k in range(chunks):
        predict(0, k)
        if k + 2 < chunks:
            transpose_volume(k + 2)
        if k == 0:
            pl.semaphore_wait(barrier, n_depth + 1)
            each_image(lambda copy: copy.start())
        send_halos(0, k)
    for k in range(chunks):
        send_parts(0, k)
    gather_images()

    for it in range(ITERS):
        for k in range(chunks):
            if it == 0 or k > 1:
                divide(it, k)
        for k in range(chunks):
            await_ratio(it, k)
            transpose_ratio(it, k)
            update(it, k)
            if it < ITERS - 1 and k > 0:
                predict(it + 1, k - 1)
                send_halos(it + 1, k - 1)
        if it < ITERS - 1:
            send_parts(it + 1, 0)
            predict(it + 1, last)
            send_halos(it + 1, last)
            send_parts(it + 1, 1)
            divide(it + 1, 0)
            send_parts(it + 1, 2)
            send_parts(it + 1, 3)
            divide(it + 1, 1)
            for k in range(chunks):
                await_part_sends(it, k)
                await_gather_sends(it, k)

    each_image(lambda copy: copy.wait_send())
    for k in range(chunks):
        await_part_sends(ITERS - 1, k)
    for k in range(chunks):
        await_gather_sends(ITERS - 1, k)
    for k in range(chunks):
        stores(k).wait()


def solution(mesh):
    n_depth, n_lat = mesh.shape["depth"], mesh.shape["lat"]

    def on_device(volume, measured, background, point_spread):
        planes, rows, cols = volume.shape
        chunks = cols // WIDTH
        steps = ITERS * chunks
        padded = cols + 2 * PAD
        vmem = lambda *shape, dtype=f32: pltpu.VMEM(shape, dtype)
        dma = lambda *shape: pltpu.SemaphoreType.DMA(shape)
        return pl.pallas_call(
            lambda *refs: kernel(n_depth, n_lat, chunks, *refs),
            out_shape=jax.ShapeDtypeStruct(volume.shape, f32),
            in_specs=[pl.BlockSpec(memory_space=pl.ANY)] * 3 + [pl.BlockSpec(memory_space=pltpu.VMEM)],
            out_specs=pl.BlockSpec(memory_space=pl.ANY),
            scratch_shapes=[
                vmem(planes, rows, cols),
                vmem(2, padded, 128),
                vmem(2, padded, 128),
                vmem(4, padded, 128),
                vmem(4, 2, WIDTH + 32, 128),
                vmem(256, 128),
                vmem(256, 256),
                vmem(256, 256, dtype=bf16),
                vmem(256, 256, dtype=bf16),
                vmem(256, 256, dtype=bf16),
                vmem(256, 256, dtype=bf16),
                vmem(ITERS, chunks, 64, WIDTH),
                vmem(ITERS, chunks, 24, WIDTH),
                vmem(ITERS, chunks, 24, WIDTH),
                vmem(ITERS, chunks, 64, WIDTH),
                vmem(ITERS, chunks, n_depth, 8, WIDTH),
                vmem(ITERS, chunks, 8, WIDTH),
                vmem(ITERS, 64, cols),
                vmem(2, rows, cols),
                vmem(2, 8, cols),
                vmem(2, 8, cols),
                vmem(2, 8, cols),
                vmem(planes, rows, cols),
                dma(chunks), dma(2), dma(chunks), pltpu.SemaphoreType.DMA, pltpu.SemaphoreType.DMA,
                dma(steps, 2), dma(steps, 2), dma(steps), dma(steps), dma(steps), dma(steps),
            ],
            compiler_params=pltpu.CompilerParams(
                collective_id=0, has_side_effects=True, vmem_limit_bytes=60 << 20
            ),
            cost_estimate=pl.CostEstimate(
                flops=2 * 3 * 4 * 4 * 2048 * 256 * 256, bytes_accessed=5 << 20, transcendentals=0
            ),
            name="deconvolve",
        )(volume, measured, background, point_spread.transpose(1, 0, 2))

    return jax.shard_map(
        on_device,
        mesh=mesh,
        in_specs=(P("depth", "lat", None), P("lat", None), P("lat", None), P("depth", None, None)),
        out_specs=P("depth", "lat", None),
        check_vma=False,
    )
```

```python
import jax
import jax.numpy as jnp
from jax import lax
from jax.experimental import pallas as pl
from jax.experimental.pallas import tpu as pltpu
from jax.sharding import PartitionSpec as P

ITERS = 2
WIDTH = 512
PAD = 32
MESH = pl.DeviceIdType.MESH
bf16, f32 = jnp.bfloat16, jnp.float32


def split(x):
    high = x.astype(bf16)
    return high, (x - high.astype(f32)).astype(bf16)


def dot3(x, w_high, w_low):
    x_high, x_low = split(x) if not isinstance(x, tuple) else x
    dot = lambda a, b: jnp.dot(a, b, preferred_element_type=f32)
    return dot(x_high, w_high[...]) + dot(x_low, w_high[...]) + dot(x_high, w_low[...])


def lanes(rows):
    return lax.broadcasted_iota(jnp.int32, (rows, 128), 1)


def quarters(rows, parts):
    lane = lanes(rows)
    first = jnp.where(lane < 32, parts[0], parts[1])
    return jnp.where(lane < 64, first, jnp.where(lane < 96, parts[2], parts[3]))


def build_weights(point_spread, taps, work, fwd_high, fwd_low, adj_high, adj_low):
    count, planes, _ = point_spread.shape
    taps[...] = jnp.zeros_like(taps)
    for a in range(count):
        taps[8 * a : 8 * a + 8, 0:count] = point_spread[a]
    row = lax.broadcasted_iota(jnp.int32, (256, 256), 0)
    col = lax.broadcasted_iota(jnp.int32, (256, 256), 1)
    flip = (row % 8 == col // 32) & (row // 8 + col % 32 == count - 1)
    flipped = lax.dot_general(
        taps[:, 0:32], flip.astype(f32), (((0,), (0,)), ((), ())),
        precision=lax.Precision.HIGHEST, preferred_element_type=f32,
    )
    column_sums = jnp.sum(flipped, axis=0, keepdims=True)
    lane = lanes(8)
    for j in range(4):
        for p in range(planes):
            half = slice(128 * (p // 4), 128 * (p // 4) + 128)
            rows = slice(8 * (planes * j + p), 8 * (planes * j + p) + 8)
            for h in range(2):
                block = jnp.zeros((8, 128), f32)
                for g in range(4 * h, min(4 * h + 4, 7)):
                    source = jnp.broadcast_to(flipped[4 * g + j : 4 * g + j + 1, half], (8, 128))
                    moved = pltpu.roll(source, 32 * (g - p) % 128, 1, stride=1, stride_axis=0)
                    block = jnp.where(lane // 32 == g % 4, moved, block)
                work[rows, 128 * h : 128 * h + 128] = block
    fwd_high[...], fwd_low[...] = split(work[...])
    for p in range(planes):
        inverse = 1.0 / jnp.sum(column_sums[:, 32 * p : 32 * p + 32], axis=1, keepdims=True)
        for j in range(4):
            rows = slice(8 * (planes * j + p), 8 * (planes * j + p) + 8)
            work[rows, :] = work[rows, :] * inverse
    adj_high[...], adj_low[...] = split(work[...].T)


def load_volume(volume, vt, vt_rolled, tile):
    cols = pl.ds(pl.multiple_of(tile * 128, 128), 128)
    rows = pl.ds(pl.multiple_of(tile * 128 + PAD, 8), 128)
    for a in range(2):
        block = jnp.concatenate(
            [volume[p, 8 * rb : 8 * rb + 8, cols] for rb in (2 * a, 2 * a + 1) for p in range(8)], 0
        ).T
        vt[a, rows, :] = block
        vt_rolled[a, rows, :] = pltpu.roll(block, 64, 1)


def forward(k, vt, vt_rolled, w_high, w_low, work, frame):
    rows = WIDTH + 32
    start = k * WIDTH
    lower = lanes(rows) < 64
    groups = [None] * 7
    for rb in range(4):
        a = rb // 2
        low, high = (vt, vt_rolled) if rb % 2 == 0 else (vt_rolled, vt)

        def pair(shift):
            return jnp.where(
                lower,
                low[a, pl.ds(start + 16 + shift, rows), :],
                high[a, pl.ds(start + 17 + shift, rows), :],
            )

        y = dot3(jnp.concatenate([pair(0), pair(2)], 1), w_high, w_low)
        work[rb, 0, 0 : WIDTH + 16, :] = y[: WIDTH + 16, :128] + y[16:, 128:]
        shifted = quarters(WIDTH, [work[rb, 0, o : o + WIDTH, :] for o in (4, 8, 12, 16)]).T
        for g in range(4):
            x = (shifted[8 * g : 8 * g + 8] + shifted[32 + 8 * g : 40 + 8 * g]) + (
                shifted[64 + 8 * g : 72 + 8 * g] + shifted[96 + 8 * g : 104 + 8 * g]
            )
            groups[rb + g] = x if groups[rb + g] is None else groups[rb + g] + x
    frame[0:56, :] = jnp.concatenate(groups, 0)
    frame[56:64, :] = jnp.zeros((8, WIDTH), f32)


def load_ratio(ratio, qt, tile, inside, rbs):
    cols = pl.ds(pl.multiple_of(tile * 128, 128), 128)
    rows = pl.ds(pl.multiple_of(tile * 128 + PAD, 8), 128)
    x = jnp.where(inside, ratio[0:56, cols], 0.0)
    for rb in rbs:
        y = x[8 * rb : 8 * rb + 32]
        qt[rb, rows, :] = jnp.concatenate([y, y, y, y], 0).T


def adjoint(start, width, qt, w_high, w_low, work, prepare):
    rows = width + 32
    lower = lanes(width) < 64
    sums = []
    for rb in range(4):
        prepare(rb)
        x = quarters(rows, [qt[rb, pl.ds(start + o, rows), :] for o in (12, 8, 4, 0)])
        both = tuple(jnp.concatenate([h[16:], h[:-16]], 1) for h in split(x))
        z = dot3(both, w_high, w_low)
        work[rb, 0, 0 : width + 16, :] = z[:, :128]
        work[rb, 1, 0 : width + 16, :] = z[:, 128:]
        sums.append(
            jnp.where(
                lower,
                work[rb, 0, 16 : 16 + width, :] + work[rb, 1, 14 : 14 + width, :],
                work[rb, 0, 15 : 15 + width, :] + work[rb, 1, 13 : 13 + width, :],
            )
        )
    return [
        jnp.where(lower, x, y) + pltpu.roll(jnp.where(lower, y, x), 64, 1)
        for x, y in ((sums[0], sums[1]), (sums[2], sums[3]))
    ]


def kernel(
    n_depth, n_lat, chunks,
    volume_hbm, measured_hbm, background_hbm, point_spread_hbm, out_hbm,
    volume, point_spread, vt, vt_rolled, qt, work, taps, w_work, fwd_high, fwd_low, adj_high, adj_low,
    frame, from_next, from_prev, total, parts, own, ratio, images, images_edge, images_halo, mine, out,
    load_sem, taps_sem, image_sem, store_sem, image_send, image_recv, halo_send, halo_recv, part_send, part_recv, gather_send, gather_recv,
):
    depth, lat = lax.axis_index("depth"), lax.axis_index("lat")
    prev, following = lax.rem(lat + n_lat - 1, n_lat), lax.rem(lat + 1, n_lat)
    has_next, has_prev = lat < n_lat - 1, lat > 0

    barrier = pltpu.get_barrier_semaphore()
    for row in (prev, following):
        pl.semaphore_signal(barrier, inc=1, device_id=(depth, row), device_id_type=MESH)
    for o in range(1, n_depth):
        pl.semaphore_signal(
            barrier, inc=1, device_id=(lax.rem(depth + o, n_depth), lat), device_id_type=MESH
        )

    def columns(k):
        return pl.ds(k * WIDTH, WIDTH)

    def group(d):
        return pl.ds(pl.multiple_of(8 * d, 8), 8)

    def loads(k):
        return pltpu.make_async_copy(volume_hbm.at[:, :, columns(k)], volume.at[:, :, columns(k)], load_sem.at[k])

    def image_loads():
        return [
            pltpu.make_async_copy(image, images.at[i], image_sem.at[i])
            for i, image in enumerate((measured_hbm, background_hbm))
        ]

    def stores(k):
        first, end = store_range(k)
        cols = pl.ds(first, end - first)
        return pltpu.make_async_copy(out.at[:, :, cols], out_hbm.at[:, :, cols], store_sem.at[k])

    taps_load = pltpu.make_async_copy(point_spread_hbm, point_spread, taps_sem)
    taps_load.start()
    for k in range(chunks):
        loads(k).start()
    for copy in image_loads():
        copy.start()

    def remote(src, dst, send, recv, device):
        return pltpu.make_async_remote_copy(
            src_ref=src, dst_ref=dst, send_sem=send, recv_sem=recv, device_id=device, device_id_type=MESH
        )

    def each_image(action):
        for g, count, neighbour in ((0, 2, following), (1, 1, following), (5, 1, prev), (6, 2, prev)):

            @pl.when(depth == g)
            def _(count=count, neighbour=neighbour):
                action(
                    remote(
                        images_edge.at[0:count], images_halo.at[0:count],
                        image_send, image_recv, (depth, neighbour),
                    )
                )

    def pack_images():
        for g, first, count in ((0, 20, 8), (1, 28, 4), (5, 0, 4), (6, 4, 8)):

            @pl.when(depth == g)
            def _(first=first, count=count):
                for i in range(2):
                    rows = images[i, first : first + count]
                    if count == 8:
                        images_edge[i] = rows
                    else:
                        images_edge[0, 4 * i : 4 * i + 4] = rows

    def gather_images():
        each_image(lambda copy: copy.wait_recv())
        for g in range(n_depth):

            @pl.when(depth == g)
            def _(g=g):
                for i in range(2):
                    if g in (0, 6):
                        mine[i] = images_halo[i]
                    elif g == 1:
                        mine[i, 0:4] = images_halo[0, 4 * i : 4 * i + 4]
                        mine[i, 4:8] = images[i, 0:4]
                    elif g == 5:
                        mine[i, 0:4] = images[i, 28:32]
                        mine[i, 4:8] = images_halo[0, 4 * i : 4 * i + 4]
                    elif g == 7:
                        mine[i] = images[i, 0:8]
                    else:
                        mine[i] = images[i, 8 * g - 12 : 8 * g - 4]

    def halo_copy(it, k, up):
        n = it * chunks + k
        if up:
            return remote(frame.at[it, k, 0:24], from_next.at[it, k], halo_send.at[n, 0], halo_recv.at[n, 0], (depth, prev))
        return remote(frame.at[it, k, 32:56], from_prev.at[it, k], halo_send.at[n, 1], halo_recv.at[n, 1], (depth, following))

    def peer(o):
        return (lax.rem(depth + o, n_depth), lat)

    def part_copy(it, k, o):
        n = it * chunks + k
        owner, _ = peer(o)
        return remote(total.at[it, k, group(owner)], parts.at[it, k, o], part_send.at[n], part_recv.at[n], peer(o))

    def gather_copy(it, k, o):
        n = it * chunks + k
        return remote(own.at[it, k], ratio.at[it, group(depth), columns(k)], gather_send.at[n], gather_recv.at[n], peer(o))

    def all_of(it, k, send, recv):
        n = it * chunks + k
        every = parts.at[it, k, 1:n_depth]
        return remote(every, every, send.at[n], recv.at[n], peer(1))

    def halos(it, k, action):
        @pl.when(has_next)
        def _():
            action(halo_copy(it, k, False))

        @pl.when(has_prev)
        def _():
            action(halo_copy(it, k, True))

    def send_halos(it, k):
        halos(it, k, lambda copy: copy.start())

    def send_parts(it, k):
        total[it, k] = frame[it, k]

        @pl.when(has_prev)
        def _():
            halo_copy(it, k, False).wait_recv()
            total[it, k, 0:24] = frame[it, k, 0:24] + from_prev[it, k]

        @pl.when(has_next)
        def _():
            halo_copy(it, k, True).wait_recv()
            total[it, k, 32:56] = frame[it, k, 32:56] + from_next[it, k]

        for o in range(1, n_depth):
            part_copy(it, k, o).start()

    def await_part_sends(it, k):
        halos(it, k, lambda copy: copy.wait_send())
        all_of(it, k, part_send, part_recv).wait_send()

    def await_gather_sends(it, k):
        all_of(it, k, gather_send, gather_recv).wait_send()

    def divide(it, k):
        all_of(it, k, part_send, part_recv).wait_recv()
        rows = group(depth)
        value = total[it, k, rows]
        for o in range(1, n_depth):
            value = value + parts[it, k, o]
        value = mine[0, :, columns(k)] / (value + mine[1, :, columns(k)])
        own[it, k] = value
        for o in range(1, n_depth):
            gather_copy(it, k, o).start()
        ratio[it, rows, columns(k)] = value

    frame_row = lax.broadcasted_iota(jnp.int32, (56, 128), 0)
    inside = ((frame_row >= 12) | (lat > 0)) & ((frame_row < 44) | (lat < n_lat - 1))

    def await_ratio(it, k):
        all_of(it, k, gather_send, gather_recv).wait_recv()

    def transpose_ratio(it, k, rb):
        for t in range(WIDTH // 128):
            load_ratio(ratio.at[it], qt, k * (WIDTH // 128) + t, inside, (rb,))

    def update_range(k):
        return max(k * WIDTH - 16, 0), (k + 1) * WIDTH - (16 if k + 1 < chunks else 0)

    def store_range(k):
        first, end = update_range(k)
        return first // 128 * 128, end // 128 * 128

    def update(it, k):
        first, end = update_range(k)
        rows = pl.ds(first + PAD, end - first)
        for a, factor in enumerate(adjoint(first, end - first, qt, adj_high, adj_low, work, lambda rb: transpose_ratio(it, k, rb))):
            value = vt[a, rows, :] * factor
            vt[a, rows, :] = value
            if it < ITERS - 1:
                vt_rolled[a, rows, :] = pltpu.roll(value, 64, 1)
        if it == ITERS - 1:
            first, end = store_range(k)
            for a in range(2):
                block = vt[a, first + PAD : end + PAD, :].T
                for i in range(16):
                    rb, p = 2 * a + i // 8, i % 8
                    out[p, 8 * rb : 8 * rb + 8, first:end] = block[8 * i : 8 * i + 8]
            stores(k).start()

    taps_load.wait()
    build_weights(point_spread, taps, w_work, fwd_high, fwd_low, adj_high, adj_low)
    tail = vt.shape[1] - PAD - chunks * WIDTH
    for ref in (vt, vt_rolled, qt):
        ref[:, 0:PAD, :] = jnp.zeros((ref.shape[0], PAD, 128), f32)
        ref[:, PAD + chunks * WIDTH :, :] = jnp.zeros((ref.shape[0], tail, 128), f32)

    def transpose_volume(k):
        for t in range(WIDTH // 128):
            load_volume(volume, vt, vt_rolled, k * (WIDTH // 128) + t)

    for copy in image_loads():
        copy.wait()
    pack_images()
    for k in range(chunks):
        loads(k).wait()
    for k in range(2):
        transpose_volume(k)

    def predict(it, k):
        forward(k, vt, vt_rolled, fwd_high, fwd_low, work, frame.at[it, k])

    last = chunks - 1
    for k in range(chunks):
        predict(0, k)
        if k + 2 < chunks:
            transpose_volume(k + 2)
        if k == 0:
            pl.semaphore_wait(barrier, n_depth + 1)
            each_image(lambda copy: copy.start())
        send_halos(0, k)
    for k in range(chunks):
        send_parts(0, k)
    gather_images()

    for it in range(ITERS):
        for k in range(chunks):
            if it == 0 or k > 1:
                divide(it, k)
        for k in range(chunks):
            await_ratio(it, k)
            update(it, k)
            if it < ITERS - 1 and k > 0:
                predict(it + 1, k - 1)
                send_halos(it + 1, k - 1)
        if it < ITERS - 1:
            send_parts(it + 1, 0)
            predict(it + 1, last)
            send_halos(it + 1, last)
            send_parts(it + 1, 1)
            divide(it + 1, 0)
            send_parts(it + 1, 2)
            send_parts(it + 1, 3)
            divide(it + 1, 1)
            for k in range(chunks):
                await_part_sends(it, k)
                await_gather_sends(it, k)

    each_image(lambda copy: copy.wait_send())
    for k in range(chunks):
        await_part_sends(ITERS - 1, k)
    for k in range(chunks):
        await_gather_sends(ITERS - 1, k)
    for k in range(chunks):
        stores(k).wait()


def solution(mesh):
    n_depth, n_lat = mesh.shape["depth"], mesh.shape["lat"]

    def on_device(volume, measured, background, point_spread):
        planes, rows, cols = volume.shape
        chunks = cols // WIDTH
        steps = ITERS * chunks
        padded = cols + 2 * PAD
        vmem = lambda *shape, dtype=f32: pltpu.VMEM(shape, dtype)
        dma = lambda *shape: pltpu.SemaphoreType.DMA(shape)
        return pl.pallas_call(
            lambda *refs: kernel(n_depth, n_lat, chunks, *refs),
            out_shape=jax.ShapeDtypeStruct(volume.shape, f32),
            in_specs=[pl.BlockSpec(memory_space=pl.ANY)] * 4,
            out_specs=pl.BlockSpec(memory_space=pl.ANY),
            scratch_shapes=[
                vmem(planes, rows, cols),
                vmem(point_spread.shape[1], planes, point_spread.shape[2]),
                vmem(2, padded, 128),
                vmem(2, padded, 128),
                vmem(4, padded, 128),
                vmem(4, 2, WIDTH + 32, 128),
                vmem(256, 128),
                vmem(256, 256),
                vmem(256, 256, dtype=bf16),
                vmem(256, 256, dtype=bf16),
                vmem(256, 256, dtype=bf16),
                vmem(256, 256, dtype=bf16),
                vmem(ITERS, chunks, 64, WIDTH),
                vmem(ITERS, chunks, 24, WIDTH),
                vmem(ITERS, chunks, 24, WIDTH),
                vmem(ITERS, chunks, 64, WIDTH),
                vmem(ITERS, chunks, n_depth, 8, WIDTH),
                vmem(ITERS, chunks, 8, WIDTH),
                vmem(ITERS, 64, cols),
                vmem(2, rows, cols),
                vmem(2, 8, cols),
                vmem(2, 8, cols),
                vmem(2, 8, cols),
                vmem(planes, rows, cols),
                dma(chunks), pltpu.SemaphoreType.DMA, dma(2), dma(chunks), pltpu.SemaphoreType.DMA, pltpu.SemaphoreType.DMA,
                dma(steps, 2), dma(steps, 2), dma(steps), dma(steps), dma(steps), dma(steps),
            ],
            compiler_params=pltpu.CompilerParams(
                collective_id=0, has_side_effects=True, vmem_limit_bytes=60 << 20
            ),
            cost_estimate=pl.CostEstimate(
                flops=2 * 3 * 4 * 4 * 2048 * 256 * 256, bytes_accessed=5 << 20, transcendentals=0
            ),
            name="deconvolve",
        )(volume, measured, background, point_spread.transpose(1, 0, 2))

    return jax.shard_map(
        on_device,
        mesh=mesh,
        in_specs=(P("depth", "lat", None), P("lat", None), P("lat", None), P("depth", None, None)),
        out_specs=P("depth", "lat", None),
        check_vma=False,
    )
```

```python
import jax
import jax.numpy as jnp
from jax import lax
from jax.experimental import pallas as pl
from jax.experimental.pallas import tpu as pltpu
from jax.sharding import PartitionSpec as P

ITERS = 2
WIDTH = 512
PAD = 32
MESH = pl.DeviceIdType.MESH
bf16, f32 = jnp.bfloat16, jnp.float32


def split(x):
    high = x.astype(bf16)
    return high, (x - high.astype(f32)).astype(bf16)


def dot3(x, w_high, w_low):
    x_high, x_low = split(x) if not isinstance(x, tuple) else x
    dot = lambda a, b: jnp.dot(a, b, preferred_element_type=f32)
    return dot(x_high, w_high[...]) + dot(x_low, w_high[...]) + dot(x_high, w_low[...])


def lanes(rows):
    return lax.broadcasted_iota(jnp.int32, (rows, 128), 1)


def quarters(rows, parts):
    lane = lanes(rows)
    first = jnp.where(lane < 32, parts[0], parts[1])
    return jnp.where(lane < 64, first, jnp.where(lane < 96, parts[2], parts[3]))


def build_weights(point_spread, taps, work, fwd_high, fwd_low, adj_high, adj_low):
    count, planes, _ = point_spread.shape
    taps[...] = jnp.zeros_like(taps)
    for a in range(count):
        taps[8 * a : 8 * a + 8, 0:count] = point_spread[a]
    row = lax.broadcasted_iota(jnp.int32, (256, 256), 0)
    col = lax.broadcasted_iota(jnp.int32, (256, 256), 1)
    flip = (row % 8 == col // 32) & (row // 8 + col % 32 == count - 1)
    flipped = lax.dot_general(
        taps[:, 0:32], flip.astype(f32), (((0,), (0,)), ((), ())),
        precision=lax.Precision.HIGHEST, preferred_element_type=f32,
    )
    column_sums = jnp.sum(flipped, axis=0, keepdims=True)
    lane = lanes(8)
    for j in range(4):
        for p in range(planes):
            half = slice(128 * (p // 4), 128 * (p // 4) + 128)
            rows = slice(8 * (planes * j + p), 8 * (planes * j + p) + 8)
            for h in range(2):
                block = jnp.zeros((8, 128), f32)
                for g in range(4 * h, min(4 * h + 4, 7)):
                    source = jnp.broadcast_to(flipped[4 * g + j : 4 * g + j + 1, half], (8, 128))
                    moved = pltpu.roll(source, 32 * (g - p) % 128, 1, stride=1, stride_axis=0)
                    block = jnp.where(lane // 32 == g % 4, moved, block)
                work[rows, 128 * h : 128 * h + 128] = block
    fwd_high[...], fwd_low[...] = split(work[...])
    for p in range(planes):
        inverse = 1.0 / jnp.sum(column_sums[:, 32 * p : 32 * p + 32], axis=1, keepdims=True)
        for j in range(4):
            rows = slice(8 * (planes * j + p), 8 * (planes * j + p) + 8)
            work[rows, :] = work[rows, :] * inverse
    adj_high[...], adj_low[...] = split(work[...].T)


def load_volume(volume, vt, vt_rolled, tile):
    cols = pl.ds(pl.multiple_of(tile * 128, 128), 128)
    rows = pl.ds(pl.multiple_of(tile * 128 + PAD, 8), 128)
    for a in range(2):
        block = jnp.concatenate(
            [volume[p, 8 * rb : 8 * rb + 8, cols] for rb in (2 * a, 2 * a + 1) for p in range(8)], 0
        ).T
        vt[a, rows, :] = block
        vt_rolled[a, rows, :] = pltpu.roll(block, 64, 1)


def forward(k, vt, vt_rolled, w_high, w_low, work, frame):
    rows = WIDTH + 32
    start = k * WIDTH
    lower = lanes(rows) < 64
    groups = [None] * 7
    for rb in range(4):
        a = rb // 2
        low, high = (vt, vt_rolled) if rb % 2 == 0 else (vt_rolled, vt)

        def pair(shift):
            return jnp.where(
                lower,
                low[a, pl.ds(start + 16 + shift, rows), :],
                high[a, pl.ds(start + 17 + shift, rows), :],
            )

        y = dot3(jnp.concatenate([pair(0), pair(2)], 1), w_high, w_low)
        work[rb, 0, 0 : WIDTH + 16, :] = y[: WIDTH + 16, :128] + y[16:, 128:]
        shifted = quarters(WIDTH, [work[rb, 0, o : o + WIDTH, :] for o in (4, 8, 12, 16)]).T
        for g in range(4):
            x = (shifted[8 * g : 8 * g + 8] + shifted[32 + 8 * g : 40 + 8 * g]) + (
                shifted[64 + 8 * g : 72 + 8 * g] + shifted[96 + 8 * g : 104 + 8 * g]
            )
            groups[rb + g] = x if groups[rb + g] is None else groups[rb + g] + x
    frame[0:56, :] = jnp.concatenate(groups, 0)
    frame[56:64, :] = jnp.zeros((8, WIDTH), f32)


def load_ratio(ratio, qt, tile, inside, rbs):
    cols = pl.ds(pl.multiple_of(tile * 128, 128), 128)
    rows = pl.ds(pl.multiple_of(tile * 128 + PAD, 8), 128)
    x = jnp.where(inside, ratio[0:56, cols], 0.0)
    for rb in rbs:
        y = x[8 * rb : 8 * rb + 32]
        qt[rb, rows, :] = jnp.concatenate([y, y, y, y], 0).T


def adjoint(start, width, qt, w_high, w_low, work, prepare):
    rows = width + 32
    lower = lanes(width) < 64
    sums = []
    for rb in range(4):
        prepare(rb)
        x = quarters(rows, [qt[rb, pl.ds(start + o, rows), :] for o in (12, 8, 4, 0)])
        both = tuple(jnp.concatenate([h[16:], h[:-16]], 1) for h in split(x))
        z = dot3(both, w_high, w_low)
        work[rb, 0, 0 : width + 16, :] = z[:, :128]
        work[rb, 1, 0 : width + 16, :] = z[:, 128:]
        sums.append(
            jnp.where(
                lower,
                work[rb, 0, 16 : 16 + width, :] + work[rb, 1, 14 : 14 + width, :],
                work[rb, 0, 15 : 15 + width, :] + work[rb, 1, 13 : 13 + width, :],
            )
        )
    return [
        jnp.where(lower, x, y) + pltpu.roll(jnp.where(lower, y, x), 64, 1)
        for x, y in ((sums[0], sums[1]), (sums[2], sums[3]))
    ]


def kernel(
    n_depth, n_lat, chunks,
    volume_hbm, measured_hbm, background_hbm, point_spread_hbm, out_hbm,
    volume, point_spread, vt, vt_rolled, qt, work, taps, w_work, fwd_high, fwd_low, adj_high, adj_low,
    frame, from_next, from_prev, total, parts, own, ratio, images, images_edge, images_halo, mine, out,
    load_sem, taps_sem, image_sem, store_sem, image_send, image_recv, halo_send, halo_recv, part_send, part_recv, gather_send, gather_recv,
):
    depth, lat = lax.axis_index("depth"), lax.axis_index("lat")
    prev, following = lax.rem(lat + n_lat - 1, n_lat), lax.rem(lat + 1, n_lat)
    has_next, has_prev = lat < n_lat - 1, lat > 0

    barrier = pltpu.get_barrier_semaphore()
    for row in (prev, following):
        pl.semaphore_signal(barrier, inc=1, device_id=(depth, row), device_id_type=MESH)
    for o in range(1, n_depth):
        pl.semaphore_signal(
            barrier, inc=1, device_id=(lax.rem(depth + o, n_depth), lat), device_id_type=MESH
        )

    def columns(k):
        return pl.ds(k * WIDTH, WIDTH)

    def group(d):
        return pl.ds(pl.multiple_of(8 * d, 8), 8)

    def loads(k):
        return pltpu.make_async_copy(volume_hbm.at[:, :, columns(k)], volume.at[:, :, columns(k)], load_sem.at[k])

    def image_loads():
        return [
            pltpu.make_async_copy(image, images.at[i], image_sem.at[i])
            for i, image in enumerate((measured_hbm, background_hbm))
        ]

    def stores(k):
        first, end = store_range(k)
        cols = pl.ds(first, end - first)
        return pltpu.make_async_copy(out.at[:, :, cols], out_hbm.at[:, :, cols], store_sem.at[k])

    taps_load = pltpu.make_async_copy(point_spread_hbm, point_spread, taps_sem)
    taps_load.start()
    for k in range(chunks):
        loads(k).start()
    for copy in image_loads():
        copy.start()

    def remote(src, dst, send, recv, device):
        return pltpu.make_async_remote_copy(
            src_ref=src, dst_ref=dst, send_sem=send, recv_sem=recv, device_id=device, device_id_type=MESH
        )

    def each_image(action):
        for g, count, neighbour in ((0, 2, following), (1, 1, following), (5, 1, prev), (6, 2, prev)):

            @pl.when(depth == g)
            def _(count=count, neighbour=neighbour):
                action(
                    remote(
                        images_edge.at[0:count], images_halo.at[0:count],
                        image_send, image_recv, (depth, neighbour),
                    )
                )

    def pack_images():
        for g, first, count in ((0, 20, 8), (1, 28, 4), (5, 0, 4), (6, 4, 8)):

            @pl.when(depth == g)
            def _(first=first, count=count):
                for i in range(2):
                    rows = images[i, first : first + count]
                    if count == 8:
                        images_edge[i] = rows
                    else:
                        images_edge[0, 4 * i : 4 * i + 4] = rows

    def gather_images():
        each_image(lambda copy: copy.wait_recv())
        for g in range(n_depth):

            @pl.when(depth == g)
            def _(g=g):
                for i in range(2):
                    if g in (0, 6):
                        mine[i] = images_halo[i]
                    elif g == 1:
                        mine[i, 0:4] = images_halo[0, 4 * i : 4 * i + 4]
                        mine[i, 4:8] = images[i, 0:4]
                    elif g == 5:
                        mine[i, 0:4] = images[i, 28:32]
                        mine[i, 4:8] = images_halo[0, 4 * i : 4 * i + 4]
                    elif g == 7:
                        mine[i] = images[i, 0:8]
                    else:
                        mine[i] = images[i, 8 * g - 12 : 8 * g - 4]

    def halo_copy(it, k, up):
        n = it * chunks + k
        if up:
            return remote(frame.at[it, k, 0:24], from_next.at[it, k], halo_send.at[n, 0], halo_recv.at[n, 0], (depth, prev))
        return remote(frame.at[it, k, 32:56], from_prev.at[it, k], halo_send.at[n, 1], halo_recv.at[n, 1], (depth, following))

    farthest_first = sorted(range(1, n_depth), key=lambda o: -min(o % 4, 4 - o % 4))

    def peer(o):
        return (lax.rem(depth + o, n_depth), lat)

    def part_copy(it, k, o):
        n = it * chunks + k
        owner, _ = peer(o)
        return remote(total.at[it, k, group(owner)], parts.at[it, k, o], part_send.at[n], part_recv.at[n], peer(o))

    def gather_copy(it, k, o):
        n = it * chunks + k
        return remote(own.at[it, k], ratio.at[it, group(depth), columns(k)], gather_send.at[n], gather_recv.at[n], peer(o))

    def all_of(it, k, send, recv):
        n = it * chunks + k
        every = parts.at[it, k, 1:n_depth]
        return remote(every, every, send.at[n], recv.at[n], peer(1))

    def halos(it, k, action):
        @pl.when(has_next)
        def _():
            action(halo_copy(it, k, False))

        @pl.when(has_prev)
        def _():
            action(halo_copy(it, k, True))

    def send_halos(it, k):
        halos(it, k, lambda copy: copy.start())

    def send_parts(it, k):
        total[it, k] = frame[it, k]

        @pl.when(has_prev)
        def _():
            halo_copy(it, k, False).wait_recv()
            total[it, k, 0:24] = frame[it, k, 0:24] + from_prev[it, k]

        @pl.when(has_next)
        def _():
            halo_copy(it, k, True).wait_recv()
            total[it, k, 32:56] = frame[it, k, 32:56] + from_next[it, k]

        for o in farthest_first:
            part_copy(it, k, o).start()

    def await_part_sends(it, k):
        halos(it, k, lambda copy: copy.wait_send())
        all_of(it, k, part_send, part_recv).wait_send()

    def await_gather_sends(it, k):
        all_of(it, k, gather_send, gather_recv).wait_send()

    def divide(it, k):
        all_of(it, k, part_send, part_recv).wait_recv()
        rows = group(depth)
        value = total[it, k, rows]
        for o in range(1, n_depth):
            value = value + parts[it, k, o]
        value = mine[0, :, columns(k)] / (value + mine[1, :, columns(k)])
        own[it, k] = value
        for o in farthest_first:
            gather_copy(it, k, o).start()
        ratio[it, rows, columns(k)] = value

    frame_row = lax.broadcasted_iota(jnp.int32, (56, 128), 0)
    inside = ((frame_row >= 12) | (lat > 0)) & ((frame_row < 44) | (lat < n_lat - 1))

    def await_ratio(it, k):
        all_of(it, k, gather_send, gather_recv).wait_recv()

    def transpose_ratio(it, k, rb):
        for t in range(WIDTH // 128):
            load_ratio(ratio.at[it], qt, k * (WIDTH // 128) + t, inside, (rb,))

    def update_range(k):
        return max(k * WIDTH - 16, 0), (k + 1) * WIDTH - (16 if k + 1 < chunks else 0)

    def store_range(k):
        first, end = update_range(k)
        return first // 128 * 128, end // 128 * 128

    def update(it, k):
        first, end = update_range(k)
        rows = pl.ds(first + PAD, end - first)
        for a, factor in enumerate(adjoint(first, end - first, qt, adj_high, adj_low, work, lambda rb: transpose_ratio(it, k, rb))):
            value = vt[a, rows, :] * factor
            vt[a, rows, :] = value
            if it < ITERS - 1:
                vt_rolled[a, rows, :] = pltpu.roll(value, 64, 1)
        if it == ITERS - 1:
            first, end = store_range(k)
            for a in range(2):
                block = vt[a, first + PAD : end + PAD, :].T
                for i in range(16):
                    rb, p = 2 * a + i // 8, i % 8
                    out[p, 8 * rb : 8 * rb + 8, first:end] = block[8 * i : 8 * i + 8]
            stores(k).start()

    taps_load.wait()
    build_weights(point_spread, taps, w_work, fwd_high, fwd_low, adj_high, adj_low)
    tail = vt.shape[1] - PAD - chunks * WIDTH
    for ref in (vt, vt_rolled, qt):
        ref[:, 0:PAD, :] = jnp.zeros((ref.shape[0], PAD, 128), f32)
        ref[:, PAD + chunks * WIDTH :, :] = jnp.zeros((ref.shape[0], tail, 128), f32)

    def transpose_volume(k):
        for t in range(WIDTH // 128):
            load_volume(volume, vt, vt_rolled, k * (WIDTH // 128) + t)

    for copy in image_loads():
        copy.wait()
    pack_images()
    for k in range(chunks):
        loads(k).wait()
    for k in range(2):
        transpose_volume(k)

    def predict(it, k):
        forward(k, vt, vt_rolled, fwd_high, fwd_low, work, frame.at[it, k])

    last = chunks - 1
    for k in range(chunks):
        predict(0, k)
        if k + 2 < chunks:
            transpose_volume(k + 2)
        if k == 0:
            pl.semaphore_wait(barrier, n_depth + 1)
            each_image(lambda copy: copy.start())
        send_halos(0, k)
    for k in range(chunks):
        send_parts(0, k)
    gather_images()

    for it in range(ITERS):
        for k in range(chunks):
            if it == 0 or k > 1:
                divide(it, k)
        for k in range(chunks):
            await_ratio(it, k)
            update(it, k)
            if it < ITERS - 1 and k > 0:
                predict(it + 1, k - 1)
                send_halos(it + 1, k - 1)
        if it < ITERS - 1:
            send_parts(it + 1, 0)
            predict(it + 1, last)
            send_halos(it + 1, last)
            send_parts(it + 1, 1)
            divide(it + 1, 0)
            send_parts(it + 1, 2)
            send_parts(it + 1, 3)
            divide(it + 1, 1)
            for k in range(chunks):
                await_part_sends(it, k)
                await_gather_sends(it, k)

    each_image(lambda copy: copy.wait_send())
    for k in range(chunks):
        await_part_sends(ITERS - 1, k)
    for k in range(chunks):
        await_gather_sends(ITERS - 1, k)
    for k in range(chunks):
        stores(k).wait()


def solution(mesh):
    n_depth, n_lat = mesh.shape["depth"], mesh.shape["lat"]

    def on_device(volume, measured, background, point_spread):
        planes, rows, cols = volume.shape
        chunks = cols // WIDTH
        steps = ITERS * chunks
        padded = cols + 2 * PAD
        vmem = lambda *shape, dtype=f32: pltpu.VMEM(shape, dtype)
        dma = lambda *shape: pltpu.SemaphoreType.DMA(shape)
        return pl.pallas_call(
            lambda *refs: kernel(n_depth, n_lat, chunks, *refs),
            out_shape=jax.ShapeDtypeStruct(volume.shape, f32),
            in_specs=[pl.BlockSpec(memory_space=pl.ANY)] * 4,
            out_specs=pl.BlockSpec(memory_space=pl.ANY),
            scratch_shapes=[
                vmem(planes, rows, cols),
                vmem(point_spread.shape[1], planes, point_spread.shape[2]),
                vmem(2, padded, 128),
                vmem(2, padded, 128),
                vmem(4, padded, 128),
                vmem(4, 2, WIDTH + 32, 128),
                vmem(256, 128),
                vmem(256, 256),
                vmem(256, 256, dtype=bf16),
                vmem(256, 256, dtype=bf16),
                vmem(256, 256, dtype=bf16),
                vmem(256, 256, dtype=bf16),
                vmem(ITERS, chunks, 64, WIDTH),
                vmem(ITERS, chunks, 24, WIDTH),
                vmem(ITERS, chunks, 24, WIDTH),
                vmem(ITERS, chunks, 64, WIDTH),
                vmem(ITERS, chunks, n_depth, 8, WIDTH),
                vmem(ITERS, chunks, 8, WIDTH),
                vmem(ITERS, 64, cols),
                vmem(2, rows, cols),
                vmem(2, 8, cols),
                vmem(2, 8, cols),
                vmem(2, 8, cols),
                vmem(planes, rows, cols),
                dma(chunks), pltpu.SemaphoreType.DMA, dma(2), dma(chunks), pltpu.SemaphoreType.DMA, pltpu.SemaphoreType.DMA,
                dma(steps, 2), dma(steps, 2), dma(steps), dma(steps), dma(steps), dma(steps),
            ],
            compiler_params=pltpu.CompilerParams(
                collective_id=0, has_side_effects=True, vmem_limit_bytes=60 << 20
            ),
            cost_estimate=pl.CostEstimate(
                flops=2 * 3 * 4 * 4 * 2048 * 256 * 256, bytes_accessed=5 << 20, transcendentals=0
            ),
            name="deconvolve",
        )(volume, measured, background, point_spread.transpose(1, 0, 2))

    return jax.shard_map(
        on_device,
        mesh=mesh,
        in_specs=(P("depth", "lat", None), P("lat", None), P("lat", None), P("depth", None, None)),
        out_specs=P("depth", "lat", None),
        check_vma=False,
    )
```
